256 devices in a mesh: wide: 32 (over y_hi, z, core), narrow: 8 (over x, y_lo).
Axes of the slice: x: 4, y: 4 (y_hi: 2, y_lo: 2; y = y_hi * 2 + y_lo), z: 8, core: 2. Of those that a mesh axis runs over, the one named last changes fastest.
Arguments:
- head_table: float32 [32768, 400], P('wide'), may hold values from -1.5 to 1.5
- head_state: float32 [32768], P('wide'), may hold values from 0.0001 to 1
- tail_table: float32 [131072, 400], P(('wide', 'narrow')), may hold values from -1.5 to 1.5
- tail_state: float32 [131072], P(('wide', 'narrow')), may hold values from 0.0001 to 1
- relations: bfloat16 [7424, 400], replicated, may hold values from -4 to 4
- head_rows: int32 [2, 262144], P(None, ('wide', 'narrow')), may hold values from 0 to 1023
- tail_rows: int32 [2, 262144], P(None, ('wide', 'narrow')), may hold values from 0 to 511
- relation_ids: int32 [2, 262144], P(None, ('wide', 'narrow')), may hold values from 0 to 7423
Outputs:
- new_head_table: float32 [32768, 400], P('wide')
- new_head_state: float32 [32768], P('wide')
- new_tail_table: float32 [131072, 400], P(('wide', 'narrow'))
- new_tail_state: float32 [131072], P(('wide', 'narrow'))
The draws below stay inside these ranges and needn't reach their ends.
All inputs are finite; a program needn't handle non-finite values.
Results may differ from the reference program's by a relative error of at most 0.01.
Values may be sent and summed in bfloat16 or wider, within the bound.
No kernel may reach another device: no remote copies, remote signals or barrier semaphores. Data moves between devices by JAX's collectives and lax.ppermute only.
A program may use at most 64 MiB of HBM per device.

```python
import math
import jax
import jax.numpy as jnp
import numpy as np
from jax import lax

D = 400
R = 7424
HROWS = 1024
TROWS = 512
EDGES = 1024
HEAD_ALL = 32768
TAIL_ALL = 131072
EDGE_ALL = 262144
N_WIDE = 32
N_NARROW = 8


def with_ends(result, rng, low, top_value):
    longest = result.shape.index(max(result.shape))
    spots = []
    for shift in (0, 1):
        where = [jax.random.randint(jax.random.fold_in(rng, axis), (), 0, length) for axis, length in enumerate(result.shape)]
        where[longest] = (where[longest] + shift) % result.shape[longest]
        spots.append(tuple(where))
    return result.at[spots[0]].set(low).at[spots[1]].set(top_value)


def steps_of(key, shape, shards, smallest, top_value):
    gain = 1.0
    for axis_at, blocks in shards:
        draws = jax.random.uniform(jax.random.fold_in(jax.random.fold_in(key, 6), axis_at), (blocks,), jnp.float32, smallest / len(shards), top_value / len(shards))
        gain = gain * jnp.repeat(jnp.exp(draws), shape[axis_at] // blocks).reshape((-1,) + (1,) * (len(shape) - 1 - axis_at))
    return gain


def cumulative_ranks(count, lean):
    loads = [(1 << 20) // math.isqrt(rank ** lean) + 1 for rank in range(1, count + 1)]
    width = 1 + sum(loads) // (1 << 30)
    return np.cumsum(np.array([max(1, weight // width) for weight in loads]))


def ranked(key, dims, count, skew):
    listing = cumulative_ranks(count, skew)
    pick = jax.random.randint(jax.random.fold_in(key, 1), dims, 0, int(listing[count - 1]))
    rank = jnp.searchsorted(jnp.asarray(listing, jnp.int32), pick, side="right")
    return jax.random.permutation(jax.random.fold_in(key, 2), count)[rank].astype(jnp.int32)


def scatter_about(stream_key, dims, deviation, most, pieces=(), kind=jnp.bfloat16):
    factor_of = steps_of(stream_key, dims, pieces, -0.22, 0.18) if pieces else 1.0
    result = jax.random.normal(stream_key, dims, jnp.float32) * deviation * factor_of
    return jnp.minimum(jnp.maximum(result, -most), most).astype(kind)


def setup_inputs(seed: int = 0) -> dict:
    key_of = jax.random.split(jax.random.key(seed), 9)
    return {
        "head_table": scatter_about(key_of[0], (HEAD_ALL, D), 0.25, 1.5, ((0, 32),), jnp.float32),
        "head_state": jnp.clip(jnp.exp(math.log(1.0) - 9.2103404 * jax.random.uniform(key_of[1], (HEAD_ALL,), jnp.float32) ** steps_of(key_of[1], (HEAD_ALL,), ((0, 32),), -0.2, 0.2)), 0.0001, 1.0),
        "tail_table": scatter_about(key_of[2], (TAIL_ALL, D), 0.25, 1.5, ((0, 256),), jnp.float32),
        "tail_state": jnp.clip(jnp.exp(math.log(1.0) - 9.2103404 * jax.random.uniform(key_of[3], (TAIL_ALL,), jnp.float32) ** steps_of(key_of[3], (TAIL_ALL,), ((0, 256),), -0.2, 0.2)), 0.0001, 1.0),
        "relations": scatter_about(key_of[4], (R, D), 1.0, 4.0),
        "head_rows": with_ends(jax.random.randint(key_of[5], (2, EDGE_ALL), 0, HROWS), jax.random.fold_in(key_of[5], 1), 0, HROWS - 1).astype(jnp.int32),
        "tail_rows": with_ends(jax.random.randint(key_of[6], (2, EDGE_ALL), 0, TROWS), jax.random.fold_in(key_of[6], 1), 0, TROWS - 1).astype(jnp.int32),
        "relation_ids": with_ends(ranked(key_of[7], (2, EDGE_ALL), R, 2), jax.random.fold_in(key_of[7], 3), 0, R - 1).astype(jnp.int32),
    }


learning = 0.1

def complex_product(first, second):
    half_width = first.shape[-1] // 2
    first_real, first_imag = (first[..., :half_width], first[..., half_width:])
    second_real, second_imag = (second[..., :half_width], second[..., half_width:])
    return jnp.concatenate([first_real * second_real - first_imag * second_imag, first_real * second_imag + first_imag * second_real], axis=-1)

def conj_product(first, second):
    half_width = first.shape[-1] // 2
    first_real, first_imag = (first[..., :half_width], first[..., half_width:])
    second_real, second_imag = (second[..., :half_width], second[..., half_width:])
    return jnp.concatenate([first_real * second_real + first_imag * second_imag, first_imag * second_real - first_real * second_imag], axis=-1)

def adagrad(table, state, grad):
    state_new = state + lax.optimization_barrier(jnp.mean(grad * grad, axis=1))
    return (table - learning * grad / jnp.sqrt(state_new)[:, None], state_new)

def edge_terms(queries, span, tail_idx):
    span_low = span.astype(jnp.bfloat16)
    row_count = span.shape[0]
    scores = jnp.dot(queries, span_low.T, preferred_element_type=jnp.float32)
    positive = tail_idx[:, None] == jnp.arange(row_count, dtype=jnp.int32)[None, :]
    slopes = jax.nn.sigmoid(scores) / row_count - jnp.where(positive, jax.nn.sigmoid(-scores), 0.0)
    slopes = slopes.astype(jnp.bfloat16)
    tail_grad = jnp.dot(slopes.T, queries, preferred_element_type=jnp.float32)
    query_grad = jnp.dot(slopes, span_low, preferred_element_type=jnp.float32).astype(jnp.bfloat16)
    return (tail_grad, query_grad)

def reference(head_table, head_state, tail_table, tail_state, relations, head_rows, tail_rows, relation_ids):
    head_tab = head_table.reshape(N_WIDE, HROWS, D)
    head_st = head_state.reshape(N_WIDE, HROWS)
    tail_tab = tail_table.reshape(N_WIDE, N_NARROW, TROWS, D)
    tail_st = tail_state.reshape(N_WIDE, N_NARROW, TROWS)
    head_idx = head_rows.reshape(2, N_WIDE, N_NARROW, EDGES)
    tail_idx = tail_rows.reshape(2, N_WIDE, N_NARROW, EDGES)
    rel_idx = relation_ids.reshape(2, N_WIDE, N_NARROW, EDGES)

    def one_group(group_items):
        table_w, state_w, spans, span_states, rows_h, rows_t, rows_r = group_items
        relation_rows = relations[rows_r].astype(jnp.float32)
        queries = complex_product(table_w[rows_h], relation_rows).astype(jnp.bfloat16)
        tail_grad, query_grad = jax.vmap(edge_terms)(queries, spans, rows_t)
        edge_grad = conj_product(query_grad.astype(jnp.float32), relation_rows)

        def add_part(grads, rows):
            return jnp.zeros(table_w.shape, jnp.float32).at[rows].add(grads)
        parts = jax.vmap(add_part)(edge_grad, rows_h)
        parts = lax.optimization_barrier(parts.astype(jnp.bfloat16)).astype(jnp.float32)
        head_grad = lax.optimization_barrier(jnp.sum(parts, axis=0))
        new_table, new_state = adagrad(table_w, state_w, head_grad)
        new_spans, new_span_states = jax.vmap(adagrad)(spans, span_states, tail_grad)
        return (new_table, new_state, new_spans, new_span_states)
    for bucket in range(2):
        rolled_tab = jnp.roll(tail_tab, bucket, axis=0)
        rolled_st = jnp.roll(tail_st, bucket, axis=0)
        head_tab, head_st, rolled_tab, rolled_st = lax.map(one_group, (head_tab, head_st, rolled_tab, rolled_st, head_idx[bucket], tail_idx[bucket], rel_idx[bucket]))
        tail_tab = jnp.roll(rolled_tab, -bucket, axis=0)
        tail_st = jnp.roll(rolled_st, -bucket, axis=0)
    return (head_tab.reshape(N_WIDE * HROWS, D), head_st.reshape(N_WIDE * HROWS), tail_tab.reshape(N_WIDE * N_NARROW * TROWS, D), tail_st.reshape(N_WIDE * N_NARROW * TROWS))
```

```python
import functools

import jax
import jax.numpy as jnp
from jax import lax
from jax.experimental import pallas as pl
from jax.experimental.pallas import tpu as pltpu
from jax.sharding import PartitionSpec as P

learning = 0.1
BF = jnp.bfloat16
F32 = jnp.float32
VMEM = pl.BlockSpec(memory_space=pltpu.VMEM)
ANY = pl.BlockSpec(memory_space=pl.ANY)
LIMIT = 48 * 1024 * 1024


def call(kernel, outs, ins, scratch=(), flops=0, nbytes=0):
    return pl.pallas_call(
        kernel,
        out_shape=[jax.ShapeDtypeStruct(s, d) for s, d in outs],
        in_specs=ins,
        out_specs=[VMEM] * len(outs),
        scratch_shapes=list(scratch),
        compiler_params=pltpu.CompilerParams(vmem_limit_bytes=LIMIT),
        cost_estimate=pl.CostEstimate(flops=flops, bytes_accessed=nbytes, transcendentals=0),
    )


def one_hot(idx, first, count):
    rows = lax.broadcasted_iota(jnp.int32, (count, idx.shape[1]), 0)
    return jnp.where(rows == idx - first, 1.0, 0.0).astype(BF)


def dot(a, b, dims=((1,), (0,))):
    return lax.dot_general(a, b, (dims, ((), ())), preferred_element_type=F32)


def relation_kernel(bucket, chunk, ids_ref, rel_hbm, out_ref, rel_ref, acc_ref, sem):
    count = rel_hbm.shape[1] // chunk

    def copy(c):
        cols = pl.ds(pl.multiple_of(c * chunk, chunk), chunk)
        return pltpu.make_async_copy(rel_hbm.at[:, cols], rel_ref.at[:, cols], sem.at[c])

    def begin(c, _):
        copy(c).start()
        return 0

    lax.fori_loop(0, count, begin, 0)
    ids = ids_ref[bucket : bucket + 1, :]
    acc_ref[...] = jnp.zeros_like(acc_ref)

    def step(c, _):
        copy(c).wait()
        cols = pl.ds(pl.multiple_of(c * chunk, chunk), chunk)
        acc_ref[...] += dot(rel_ref[:, cols], one_hot(ids, c * chunk, chunk))
        return 0

    lax.fori_loop(0, count, step, 0)
    out_ref[...] = acc_ref[...].astype(BF)


def gather_relations(bucket, ids, rel_t):
    chunk = 256
    depth, types = rel_t.shape
    edges = ids.shape[1]
    return call(
        functools.partial(relation_kernel, bucket, chunk),
        [((depth, edges), BF)],
        [VMEM, ANY],
        [
            pltpu.VMEM((depth, types), BF),
            pltpu.VMEM((depth, edges), F32),
            pltpu.SemaphoreType.DMA((types // chunk,)),
        ],
        flops=2 * depth * types * edges,
        nbytes=2 * depth * types,
    )(ids, rel_t)[0]


def edge_work(bucket, head, span_low, rel_ref, rows_ref, tails_ref, part_ref, q_ref, sl_ref, hot_ref):
    half = head.shape[0] // 2
    hrows = head.shape[1]
    trows = span_low.shape[1]
    hot_ref[...] = one_hot(rows_ref[bucket : bucket + 1, :], 0, hrows)
    high = head.astype(BF)
    low = (head - high.astype(F32)).astype(BF)
    h = dot(high, hot_ref[...]) + dot(low, hot_ref[...])
    r = rel_ref[...].astype(F32)
    h_re, h_im, r_re, r_im = h[:half], h[half:], r[:half], r[half:]
    q_ref[...] = jnp.concatenate(
        [h_re * r_re - h_im * r_im, h_re * r_im + h_im * r_re], axis=0
    ).astype(BF)
    scores = dot(span_low, q_ref[...], ((0,), (0,)))
    soft = jnp.tanh(0.5 * scores) * 0.5 + 0.5
    at = lax.broadcasted_iota(jnp.int32, scores.shape, 0) == tails_ref[bucket : bucket + 1, :]
    sl_ref[...] = jnp.where(at, soft * (1.0 / trows) - (1.0 - soft), soft * (1.0 / trows)).astype(BF)
    g = dot(span_low, sl_ref[...])
    g_re, g_im = g[:half], g[half:]
    edge = jnp.concatenate(
        [g_re * r_re + g_im * r_im, g_im * r_re - g_re * r_im], axis=0
    ).astype(BF)
    part = dot(edge, hot_ref[...], ((1,), (1,))).astype(BF)
    width = part_ref.shape[2]
    for n in range(part_ref.shape[0]):
        part_ref[n] = part[:, n * width : (n + 1) * width]


def first_kernel(head_ref, tail_ref, rel_ref, rows_ref, tails_ref, part_ref, q_ref, sl_ref, hot_ref):
    edge_work(
        0, head_ref[...], tail_ref[...].astype(BF), rel_ref, rows_ref, tails_ref, part_ref, q_ref, sl_ref, hot_ref
    )


def stepped(table, state, grad):
    state_new = state + jnp.sum(grad * grad, axis=0, keepdims=True) * (1.0 / grad.shape[0])
    return table - (learning * lax.rsqrt(state_new)) * grad, state_new


def joined(sums_ref):
    return jnp.concatenate([sums_ref[n] for n in range(sums_ref.shape[0])], axis=1).astype(F32)


def second_kernel(
    head_ref, state_ref, sums_ref, span_ref, rel_ref, rows_ref, tails_ref,
    part_ref, q_ref, sl_ref, head_out, state_out, hot_ref,
):
    head, state = stepped(head_ref[...], state_ref[...], joined(sums_ref))
    head_out[...] = head
    state_out[...] = state
    edge_work(1, head, span_ref[...], rel_ref, rows_ref, tails_ref, part_ref, q_ref, sl_ref, hot_ref)


def tail_kernel(q_ref, sl_ref, tail_ref, state_ref, tail_out, state_out, low_out):
    grad = dot(q_ref[...], sl_ref[...], ((1,), (1,)))
    tail, state = stepped(tail_ref[...], state_ref[...], grad)
    tail_out[...] = tail
    state_out[...] = state
    low_out[...] = tail.astype(BF)


def grad_kernel(q_ref, sl_ref, grad_out):
    grad_out[...] = dot(q_ref[...], sl_ref[...], ((1,), (1,))).astype(BF)


def tail_end_kernel(tail_ref, state_ref, grad_ref, tail_out, state_out):
    tail_out[...], state_out[...] = stepped(tail_ref[...], state_ref[...], grad_ref[...].astype(F32))


def head_end_kernel(head_ref, state_ref, sums_ref, head_out, state_out):
    head_out[...], state_out[...] = stepped(head_ref[...], state_ref[...], joined(sums_ref))


def passed_along(value, axis, steps):
    count = lax.axis_size(axis)
    return lax.ppermute(value, axis, [(source, (source + steps) % count) for source in range(count)])


def summed(part):
    got = lax.all_to_all(part, "narrow", 0, 0, tiled=True)
    mine = jnp.sum(got.astype(F32), axis=0).astype(BF)
    return lax.all_to_all(jnp.broadcast_to(mine[None], part.shape), "narrow", 0, 0, tiled=True)


def local(head_table, head_state, tail_table, tail_state, relations, head_rows, tail_rows, relation_ids):
    head, tail, rel = head_table.T, tail_table.T, relations.T
    h_state, t_state = head_state[None], tail_state[None]
    depth, hrows = head.shape
    trows = tail.shape[1]
    edges = head_rows.shape[1]
    groups = lax.axis_size("narrow")
    edge_outs = [((groups, depth, hrows // groups), BF), ((depth, edges), BF), ((trows, edges), BF)]
    hot = [pltpu.VMEM((hrows, edges), BF)]
    edge_flops = 2 * depth * edges * (2 * trows + 3 * hrows)

    rel_0 = gather_relations(0, relation_ids, rel)
    part, q, slopes = call(first_kernel, edge_outs, [VMEM] * 5, hot, edge_flops, 8 << 20)(
        head, tail, rel_0, head_rows, tail_rows
    )
    tail, t_state, low = call(
        tail_kernel, [((depth, trows), F32), ((1, trows), F32), ((depth, trows), BF)], [VMEM] * 4,
        (), 2 * depth * edges * trows, 4 << 20,
    )(q, slopes, tail, t_state)
    rel_1 = gather_relations(1, relation_ids, rel)
    low = passed_along(low, "wide", 1)
    sums = summed(part)
    part, q, slopes, head, h_state = call(
        second_kernel, edge_outs + [((depth, hrows), F32), ((1, hrows), F32)], [VMEM] * 7, hot, edge_flops, 9 << 20
    )(head, h_state, sums, low, rel_1, head_rows, tail_rows)
    grad = call(grad_kernel, [((depth, trows), BF)], [VMEM] * 2, (), 2 * depth * edges * trows, 2 << 20)(q, slopes)[0]
    grad = passed_along(grad, "wide", -1)
    sums = summed(part)
    tail, t_state = call(
        tail_end_kernel, [((depth, trows), F32), ((1, trows), F32)], [VMEM] * 3, (), 0, 2 << 20
    )(tail, t_state, grad)
    head, h_state = call(
        head_end_kernel, [((depth, hrows), F32), ((1, hrows), F32)], [VMEM] * 3, (), 0, 4 << 20
    )(head, h_state, sums)
    return head.T, h_state[0], tail.T, t_state[0]


def solution(mesh):
    return jax.shard_map(
        local,
        mesh=mesh,
        in_specs=(
            P("wide", None),
            P("wide"),
            P(("wide", "narrow"), None),
            P(("wide", "narrow")),
            P(),
            P(None, ("wide", "narrow")),
            P(None, ("wide", "narrow")),
            P(None, ("wide", "narrow")),
        ),
        out_specs=(P("wide", None), P("wide"), P(("wide", "narrow"), None), P(("wide", "narrow"))),
        check_vma=False,
    )
```

```python
import functools

import jax
import jax.numpy as jnp
from jax import lax
from jax.experimental import pallas as pl
from jax.experimental.pallas import tpu as pltpu
from jax.sharding import PartitionSpec as P

learning = 0.1
BF = jnp.bfloat16
F32 = jnp.float32
VMEM = pl.BlockSpec(memory_space=pltpu.VMEM)
ANY = pl.BlockSpec(memory_space=pl.ANY)
LANES = 128
TILE = 512
PIECES = 8


def call(kernel, outs, ins, scratch=(), mib=32, flops=0, nbytes=0, out_specs=None):
    return pl.pallas_call(
        kernel,
        out_shape=[jax.ShapeDtypeStruct(s, d) for s, d in outs],
        in_specs=ins,
        out_specs=out_specs or [VMEM] * len(outs),
        scratch_shapes=list(scratch),
        compiler_params=pltpu.CompilerParams(vmem_limit_bytes=mib << 20),
        cost_estimate=pl.CostEstimate(flops=flops, bytes_accessed=nbytes, transcendentals=0),
    )


def one_hot(idx, first, count):
    rows = lax.broadcasted_iota(jnp.int32, (count, idx.shape[1]), 0)
    return jnp.where(rows == idx - first, 1.0, 0.0).astype(BF)


def dot(a, b, dims=((1,), (0,))):
    return lax.dot_general(a, b, (dims, ((), ())), preferred_element_type=F32)


def pieces_of(width):
    blocks = width // LANES
    each = -(-blocks // PIECES)
    return [(p * each * LANES, min(each, blocks - p * each) * LANES) for p in range(PIECES)]


def relation_copies(rel_hbm, rel_ref, sem):
    return [
        pltpu.make_async_copy(rel_hbm.at[:, pl.ds(a, n)], rel_ref.at[:, pl.ds(a, n)], sem.at[p])
        for p, (a, n) in enumerate(pieces_of(rel_hbm.shape[1]))
    ]


def relation_tile(rel_ref, ids, copies):
    total = None
    for p, (a, n) in enumerate(pieces_of(rel_ref.shape[1])):
        if copies is not None:
            copies[p].wait()
        term = dot(rel_ref[:, a : a + n], one_hot(ids, a, n))
        total = term if total is None else total + term
    return total


def relation_kernel(bucket, ids_ref, rel_hbm, out_ref, rel_ref, sem):
    copies = relation_copies(rel_hbm, rel_ref, sem)
    for copy in copies:
        copy.start()
    for t in range(ids_ref.shape[1] // TILE):
        cols = pl.ds(t * TILE, TILE)
        out_ref[:, cols] = relation_tile(rel_ref, ids_ref[bucket : bucket + 1, cols], None if t else copies).astype(BF)


def edge_tile(h, r, low, tails):
    half = h.shape[0] // 2
    h_re, h_im, r_re, r_im = h[:half], h[half:], r[:half], r[half:]
    q = jnp.concatenate([h_re * r_re - h_im * r_im, h_re * r_im + h_im * r_re], axis=0).astype(BF)
    t = jnp.tanh(0.5 * dot(low, q, ((0,), (0,))))
    at = lax.broadcasted_iota(jnp.int32, t.shape, 0) == tails
    k = 0.5 / low.shape[1]
    slopes = jnp.where(at, t * (k + 0.5) + (k - 0.5), t * k + k).astype(BF)
    g = dot(low, slopes)
    g_re, g_im = g[:half], g[half:]
    edge = jnp.concatenate([g_re * r_re + g_im * r_im, g_im * r_re - g_re * r_im], axis=0).astype(BF)
    return q, slopes, edge


def scatter(part_ref, edge_ref, hot_ref):
    width = part_ref.shape[2]
    for n in range(part_ref.shape[0]):
        part_ref[n] = dot(edge_ref[...], hot_ref[n * width : (n + 1) * width, :], ((1,), (1,))).astype(BF)


def stepped(table, state, grad):
    state_new = state + jnp.sum(grad * grad, axis=0, keepdims=True) * (1.0 / grad.shape[0])
    return table - (learning * lax.rsqrt(state_new)) * grad, state_new


def first_kernel(
    head_hbm, tail_hbm, rel_hbm, rows_hbm, tails_hbm, ids_hbm, state_ref, part_ref, tail_out, state_out, low_out,
    head_ref, tail_ref, rel_ref, rows_ref, tails_ref, ids_ref, hot_ref, low_ref, h_ref, edge_ref, q_ref, sl_ref, sem, rel_sem,
):
    pairs = [(rows_hbm, rows_ref), (ids_hbm, ids_ref), (head_hbm, head_ref), (tails_hbm, tails_ref), (tail_hbm, tail_ref)]
    copies = [pltpu.make_async_copy(a, b, sem.at[i]) for i, (a, b) in enumerate(pairs)]
    rel_copies = relation_copies(rel_hbm, rel_ref, rel_sem)
    for copy in copies + rel_copies:
        copy.start()
    copies[0].wait()
    hot_ref[...] = one_hot(rows_ref[0:1, :], 0, head_ref.shape[1])
    copies[1].wait()
    copies[2].wait()
    h_ref[...] = dot(head_ref[...].astype(BF), hot_ref[...])
    copies[3].wait()
    copies[4].wait()
    low_ref[...] = tail_ref[...].astype(BF)
    for t in range(ids_ref.shape[1] // TILE):
        cols = pl.ds(t * TILE, TILE)
        r = relation_tile(rel_ref, ids_ref[0:1, cols], None if t else rel_copies)
        q_ref[:, cols], sl_ref[:, cols], edge_ref[:, cols] = edge_tile(
            h_ref[:, cols], r, low_ref[...], tails_ref[0:1, cols]
        )
    scatter(part_ref, edge_ref, hot_ref)
    tail, state_out[...] = stepped(tail_ref[...], state_ref[...], dot(q_ref[...], sl_ref[...], ((1,), (1,))))
    tail_out[...] = tail
    low_out[...] = tail.astype(BF)


def sum_kernel(got_ref, out_ref):
    total = got_ref[0].astype(F32)
    for n in range(1, got_ref.shape[0]):
        total = total + got_ref[n].astype(F32)
    total = total.astype(BF)
    for n in range(out_ref.shape[0]):
        out_ref[n] = total


def second_kernel(
    head_ref, state_ref, sums_ref, low_ref, rel_ref, rows_ref, tails_ref, part_ref, grad_out,
    head_low, hot_ref, edge_ref, q_ref, sl_ref,
):
    groups, _, width = sums_ref.shape
    for n in range(groups):
        cols = pl.ds(n * width, width)
        head_low[:, cols] = stepped(head_ref[:, cols], state_ref[:, cols], sums_ref[n].astype(F32))[0].astype(BF)
    hot_ref[...] = one_hot(rows_ref[1:2, :], 0, head_ref.shape[1])
    for t in range(rows_ref.shape[1] // TILE):
        cols = pl.ds(t * TILE, TILE)
        h = dot(head_low[...], hot_ref[:, cols])
        q_ref[:, cols], sl_ref[:, cols], edge_ref[:, cols] = edge_tile(
            h, rel_ref[:, cols].astype(F32), low_ref[...], tails_ref[1:2, cols]
        )
    scatter(part_ref, edge_ref, hot_ref)
    grad_out[...] = dot(q_ref[...], sl_ref[...], ((1,), (1,))).astype(BF)


def tail_end_kernel(tail_ref, state_ref, grad_ref, tail_out, state_out):
    tail_out[...], state_out[...] = stepped(tail_ref[...], state_ref[...], grad_ref[...].astype(F32))


def head_kernel(head_ref, state_ref, sums_ref, head_out, state_out):
    groups, _, width = sums_ref.shape
    for n in range(groups):
        cols = pl.ds(n * width, width)
        head_out[:, cols], state_out[:, cols] = stepped(
            head_ref[:, cols], state_ref[:, cols], sums_ref[n].astype(F32)
        )


def passed_along(value, axis, steps):
    count = lax.axis_size(axis)
    return lax.ppermute(value, axis, [(source, (source + steps) % count) for source in range(count)])


def spread(got, *before):
    same = call(sum_kernel, [(got.shape, BF)], [VMEM], (), 24, 0, 2 << 20)(got)[0]
    same, *before = lax.optimization_barrier((same, *before))
    return lax.all_to_all(same, "narrow", 0, 0, tiled=True), *before


def local(head_table, head_state, tail_table, tail_state, relations, head_rows, tail_rows, relation_ids):
    head, tail, rel = head_table.T, tail_table.T, relations.T
    h_state, t_state = head_state[None], tail_state[None]
    depth, hrows = head.shape
    types = rel.shape[1]
    trows = tail.shape[1]
    edges = head_rows.shape[1]
    groups = lax.axis_size("narrow")
    width = hrows // groups
    part_out = ((groups, depth, width), BF)
    edge_flops = 2 * depth * edges * (3 * trows + 2 * hrows)
    rel_flops = 2 * depth * types * edges
    ints = pltpu.VMEM(head_rows.shape, jnp.int32)
    hot = pltpu.VMEM((hrows, edges), BF)
    edge = pltpu.VMEM((depth, edges), BF)
    slope = pltpu.VMEM((trows, edges), BF)
    rel_scratch = pltpu.VMEM(rel.shape, BF)
    rel_sem = pltpu.SemaphoreType.DMA((PIECES,))

    part, tail, t_state, low = call(
        first_kernel, [part_out, (tail.shape, F32), ((1, trows), F32), (tail.shape, BF)], [ANY] * 6 + [VMEM],
        [
            pltpu.VMEM(head.shape, F32), pltpu.VMEM(tail.shape, F32), rel_scratch, ints, ints, ints,
            hot, pltpu.VMEM(tail.shape, BF), pltpu.VMEM((depth, edges), F32), edge, edge, slope,
            pltpu.SemaphoreType.DMA((5,)), rel_sem,
        ],
        60, edge_flops + rel_flops, 12 << 20,
    )(head, tail, rel, head_rows, tail_rows, relation_ids, t_state)
    got = lax.all_to_all(part, "narrow", 0, 0, tiled=True)
    rel_1 = call(
        functools.partial(relation_kernel, 1), [((depth, edges), BF)], [VMEM, ANY], [rel_scratch, rel_sem],
        60, rel_flops, 2 * depth * types,
    )(relation_ids, rel)[0]
    moved = passed_along(low, "wide", 1)
    sums, moved, rel_1, tail, t_state = spread(got, moved, rel_1, tail, t_state)
    part, grad = call(
        second_kernel, [part_out, (tail.shape, BF)], [VMEM] * 7,
        [pltpu.VMEM(head.shape, BF), hot, edge, edge, slope],
        24, edge_flops, 9 << 20,
    )(head, h_state, sums, moved, rel_1, head_rows, tail_rows)
    got = lax.all_to_all(part, "narrow", 0, 0, tiled=True)
    grad = passed_along(grad, "wide", -1)
    head_step = call(
        head_kernel, [(head.shape, F32), ((1, hrows), F32)], [VMEM] * 3, (), 24, 0, 4 << 20
    )
    head, h_state = head_step(head, h_state, sums)
    tail, t_state = call(
        tail_end_kernel, [(tail.shape, F32), ((1, trows), F32)], [VMEM] * 3, (), 24, 0, 2 << 20
    )(tail, t_state, grad)
    sums, tail, t_state, head, h_state = spread(got, tail, t_state, head, h_state)
    head, h_state = head_step(head, h_state, sums)
    return head.T, h_state[0], tail.T, t_state[0]


def solution(mesh):
    return jax.shard_map(
        local,
        mesh=mesh,
        in_specs=(
            P("wide", None),
            P("wide"),
            P(("wide", "narrow"), None),
            P(("wide", "narrow")),
            P(),
            P(None, ("wide", "narrow")),
            P(None, ("wide", "narrow")),
            P(None, ("wide", "narrow")),
        ),
        out_specs=(P("wide", None), P("wide"), P(("wide", "narrow"), None), P(("wide", "narrow"))),
        check_vma=False,
    )
```

```python
import functools

import jax
import jax.numpy as jnp
from jax import lax
from jax.experimental import pallas as pl
from jax.experimental.pallas import tpu as pltpu
from jax.sharding import PartitionSpec as P

learning = 0.1
BF = jnp.bfloat16
F32 = jnp.float32
VMEM = pl.BlockSpec(memory_space=pltpu.VMEM)
ANY = pl.BlockSpec(memory_space=pl.ANY)
LANES = 128
TILE = 1024
CUTS = (4, 12, 30)
PIECES = len(CUTS) + 1
SPAN = 512


def call(kernel, outs, ins, scratch=(), mib=32, flops=0, nbytes=0, out_specs=None):
    return pl.pallas_call(
        kernel,
        out_shape=[jax.ShapeDtypeStruct(s, d) for s, d in outs],
        in_specs=ins,
        out_specs=out_specs or [VMEM] * len(outs),
        scratch_shapes=list(scratch),
        compiler_params=pltpu.CompilerParams(vmem_limit_bytes=mib << 20),
        cost_estimate=pl.CostEstimate(flops=flops, bytes_accessed=nbytes, transcendentals=0),
    )


def one_hot(idx, first, count):
    rows = lax.broadcasted_iota(jnp.int32, (count, idx.shape[1]), 0)
    return jnp.where(rows == idx - first, 1.0, 0.0).astype(BF)


def dot(a, b, dims=((1,), (0,))):
    return lax.dot_general(a, b, (dims, ((), ())), preferred_element_type=F32)


def pieces_of(width):
    ends = [0, *(c * LANES for c in CUTS), width]
    return [(a, b - a) for a, b in zip(ends, ends[1:])]


def relation_copies(rel_hbm, rel_ref, sem):
    return [
        pltpu.make_async_copy(rel_hbm.at[:, pl.ds(a, n)], rel_ref.at[:, pl.ds(a, n)], sem.at[p])
        for p, (a, n) in enumerate(pieces_of(rel_hbm.shape[1]))
    ]


def relation_tile(rel_ref, ids, copies):
    total = None
    for p, (a, n) in enumerate(pieces_of(rel_ref.shape[1])):
        if copies is not None:
            copies[p].wait()
        term = dot(rel_ref[:, a : a + n], one_hot(ids, a, n))
        total = term if total is None else total + term
    return total


def relation_kernel(bucket, ids_ref, rel_hbm, out_ref, rel_ref, sem):
    copies = relation_copies(rel_hbm, rel_ref, sem)
    for copy in copies:
        copy.start()
    for t in range(ids_ref.shape[1] // TILE):
        cols = pl.ds(t * TILE, TILE)
        out_ref[:, cols] = relation_tile(rel_ref, ids_ref[bucket : bucket + 1, cols], None if t else copies).astype(BF)


def edge_tile(h, r, low, tails):
    half = h.shape[0] // 2
    h_re, h_im, r_re, r_im = h[:half], h[half:], r[:half], r[half:]
    q = jnp.concatenate([h_re * r_re - h_im * r_im, h_re * r_im + h_im * r_re], axis=0).astype(BF)
    t = jnp.tanh(0.5 * dot(low, q, ((0,), (0,))))
    at = lax.broadcasted_iota(jnp.int32, t.shape, 0) == tails
    k = 0.5 / low.shape[1]
    slopes = jnp.where(at, t * (k + 0.5) + (k - 0.5), t * k + k).astype(BF)
    g = dot(low, slopes)
    g_re, g_im = g[:half], g[half:]
    edge = jnp.concatenate([g_re * r_re + g_im * r_im, g_im * r_re - g_re * r_im], axis=0).astype(BF)
    return q, slopes, edge


def scatter(part_ref, edge_ref, hot_ref):
    width = part_ref.shape[2]
    for first in range(0, hot_ref.shape[0], SPAN):
        part = dot(edge_ref[...], hot_ref[first : first + SPAN, :], ((1,), (1,))).astype(BF)
        for n in range(SPAN // width):
            part_ref[first // width + n] = part[:, n * width : (n + 1) * width]


def stepped(table, state, grad):
    state_new = state + jnp.sum(grad * grad, axis=0, keepdims=True) * (1.0 / grad.shape[0])
    return table - (learning * lax.rsqrt(state_new)) * grad, state_new


def first_kernel(
    head_hbm, tail_hbm, rel_hbm, rows_hbm, tails_hbm, ids_hbm, state_ref, part_ref, tail_out, state_out, low_out,
    head_ref, tail_ref, rel_ref, rows_ref, tails_ref, ids_ref, hot_ref, low_ref, h_ref, edge_ref, q_ref, sl_ref, sem, rel_sem,
):
    pairs = [(ids_hbm, ids_ref), (rows_hbm, rows_ref), (head_hbm, head_ref), (tails_hbm, tails_ref), (tail_hbm, tail_ref)]
    copies = [pltpu.make_async_copy(a, b, sem.at[i]) for i, (a, b) in enumerate(pairs)]
    rel_copies = relation_copies(rel_hbm, rel_ref, rel_sem)
    for copy in copies[:1] + rel_copies + copies[1:]:
        copy.start()
    copies[0].wait()
    r = relation_tile(rel_ref, ids_ref[0:1, :], rel_copies)
    for copy in copies[1:]:
        copy.wait()
    hot_ref[...] = one_hot(rows_ref[0:1, :], 0, head_ref.shape[1])
    h = dot(head_ref[...].astype(BF), hot_ref[...])
    low_ref[...] = tail_ref[...].astype(BF)
    q_ref[...], sl_ref[...], edge_ref[...] = edge_tile(h, r, low_ref[...], tails_ref[0:1, :])
    scatter(part_ref, edge_ref, hot_ref)
    tail, state_out[...] = stepped(tail_ref[...], state_ref[...], dot(q_ref[...], sl_ref[...], ((1,), (1,))))
    tail_out[...] = tail
    low_out[...] = tail.astype(BF)


def sum_kernel(got_ref, out_ref):
    total = got_ref[0].astype(F32)
    for n in range(1, got_ref.shape[0]):
        total = total + got_ref[n].astype(F32)
    total = total.astype(BF)
    for n in range(out_ref.shape[0]):
        out_ref[n] = total


def second_kernel(
    head_ref, state_ref, sums_ref, low_ref, rel_ref, rows_ref, tails_ref, part_ref, grad_out,
    head_low, hot_ref, edge_ref, q_ref, sl_ref,
):
    groups, _, width = sums_ref.shape
    for n in range(groups):
        cols = pl.ds(n * width, width)
        head_low[:, cols] = stepped(head_ref[:, cols], state_ref[:, cols], sums_ref[n].astype(F32))[0].astype(BF)
    hot_ref[...] = one_hot(rows_ref[1:2, :], 0, head_ref.shape[1])
    for t in range(rows_ref.shape[1] // TILE):
        cols = pl.ds(t * TILE, TILE)
        h = dot(head_low[...], hot_ref[:, cols])
        q_ref[:, cols], sl_ref[:, cols], edge_ref[:, cols] = edge_tile(
            h, rel_ref[:, cols].astype(F32), low_ref[...], tails_ref[1:2, cols]
        )
    scatter(part_ref, edge_ref, hot_ref)
    grad_out[...] = dot(q_ref[...], sl_ref[...], ((1,), (1,))).astype(BF)


def tail_end_kernel(tail_ref, state_ref, grad_ref, tail_out, state_out):
    tail_out[...], state_out[...] = stepped(tail_ref[...], state_ref[...], grad_ref[...].astype(F32))


def head_kernel(head_ref, state_ref, sums_ref, head_out, state_out):
    groups, _, width = sums_ref.shape
    for n in range(groups):
        cols = pl.ds(n * width, width)
        head_out[:, cols], state_out[:, cols] = stepped(
            head_ref[:, cols], state_ref[:, cols], sums_ref[n].astype(F32)
        )


def passed_along(value, axis, steps):
    count = lax.axis_size(axis)
    return lax.ppermute(value, axis, [(source, (source + steps) % count) for source in range(count)])


def spread(got, *before):
    same = call(sum_kernel, [(got.shape, BF)], [VMEM], (), 24, 0, 2 << 20)(got)[0]
    same, *before = lax.optimization_barrier((same, *before))
    return lax.all_to_all(same, "narrow", 0, 0, tiled=True), *before


def local(head_table, head_state, tail_table, tail_state, relations, head_rows, tail_rows, relation_ids):
    head, tail, rel = head_table.T, tail_table.T, relations.T
    h_state, t_state = head_state[None], tail_state[None]
    depth, hrows = head.shape
    types = rel.shape[1]
    trows = tail.shape[1]
    edges = head_rows.shape[1]
    groups = lax.axis_size("narrow")
    width = hrows // groups
    part_out = ((groups, depth, width), BF)
    edge_flops = 2 * depth * edges * (3 * trows + 2 * hrows)
    rel_flops = 2 * depth * types * edges
    ints = pltpu.VMEM(head_rows.shape, jnp.int32)
    hot = pltpu.VMEM((hrows, edges), BF)
    edge = pltpu.VMEM((depth, edges), BF)
    slope = pltpu.VMEM((trows, edges), BF)
    rel_scratch = pltpu.VMEM(rel.shape, BF)
    rel_sem = pltpu.SemaphoreType.DMA((PIECES,))

    part, tail, t_state, low = call(
        first_kernel, [part_out, (tail.shape, F32), ((1, trows), F32), (tail.shape, BF)], [ANY] * 6 + [VMEM],
        [
            pltpu.VMEM(head.shape, F32), pltpu.VMEM(tail.shape, F32), rel_scratch, ints, ints, ints,
            hot, pltpu.VMEM(tail.shape, BF), pltpu.VMEM((depth, edges), F32), edge, edge, slope,
            pltpu.SemaphoreType.DMA((5,)), rel_sem,
        ],
        60, edge_flops + rel_flops, 12 << 20,
    )(head, tail, rel, head_rows, tail_rows, relation_ids, t_state)
    got = lax.all_to_all(part, "narrow", 0, 0, tiled=True)
    rel_1 = call(
        functools.partial(relation_kernel, 1), [((depth, edges), BF)], [VMEM, ANY], [rel_scratch, rel_sem],
        60, rel_flops, 2 * depth * types,
    )(relation_ids, rel)[0]
    moved = passed_along(low, "wide", 1)
    sums, moved, rel_1, tail, t_state = spread(got, moved, rel_1, tail, t_state)
    part, grad = call(
        second_kernel, [part_out, (tail.shape, BF)], [VMEM] * 7,
        [pltpu.VMEM(head.shape, BF), hot, edge, edge, slope],
        24, edge_flops, 9 << 20,
    )(head, h_state, sums, moved, rel_1, head_rows, tail_rows)
    got = lax.all_to_all(part, "narrow", 0, 0, tiled=True)
    grad = passed_along(grad, "wide", -1)
    head_step = call(
        head_kernel, [(head.shape, F32), ((1, hrows), F32)], [VMEM] * 3, (), 24, 0, 4 << 20
    )
    head, h_state = head_step(head, h_state, sums)
    tail, t_state = call(
        tail_end_kernel, [(tail.shape, F32), ((1, trows), F32)], [VMEM] * 3, (), 24, 0, 2 << 20
    )(tail, t_state, grad)
    sums, tail, t_state, head, h_state = spread(got, tail, t_state, head, h_state)
    head, h_state = head_step(head, h_state, sums)
    return head.T, h_state[0], tail.T, t_state[0]


def solution(mesh):
    return jax.shard_map(
        local,
        mesh=mesh,
        in_specs=(
            P("wide", None),
            P("wide"),
            P(("wide", "narrow"), None),
            P(("wide", "narrow")),
            P(),
            P(None, ("wide", "narrow")),
            P(None, ("wide", "narrow")),
            P(None, ("wide", "narrow")),
        ),
        out_specs=(P("wide", None), P("wide"), P(("wide", "narrow"), None), P(("wide", "narrow"))),
        check_vma=False,
    )
```

```python
import functools

import jax
import jax.numpy as jnp
from jax import lax
from jax.experimental import pallas as pl
from jax.experimental.pallas import tpu as pltpu
from jax.sharding import PartitionSpec as P

learning = 0.1
BF = jnp.bfloat16
F32 = jnp.float32
VMEM = pl.BlockSpec(memory_space=pltpu.VMEM)
ANY = pl.BlockSpec(memory_space=pl.ANY)
LANES = 128
TILE = 1024
CUTS = (4, 12, 30)
PIECES = len(CUTS) + 1
SPAN = 512


def call(kernel, outs, ins, scratch=(), mib=32, flops=0, nbytes=0, out_specs=None):
    return pl.pallas_call(
        kernel,
        out_shape=[jax.ShapeDtypeStruct(s, d) for s, d in outs],
        in_specs=ins,
        out_specs=out_specs or [VMEM] * len(outs),
        scratch_shapes=list(scratch),
        compiler_params=pltpu.CompilerParams(vmem_limit_bytes=mib << 20),
        cost_estimate=pl.CostEstimate(flops=flops, bytes_accessed=nbytes, transcendentals=0),
    )


def one_hot(idx, first, count):
    rows = lax.broadcasted_iota(jnp.int32, (count, idx.shape[1]), 0)
    return jnp.where(rows == idx - first, 1.0, 0.0).astype(BF)


def dot(a, b, dims=((1,), (0,))):
    return lax.dot_general(a, b, (dims, ((), ())), preferred_element_type=F32)


def pieces_of(width):
    ends = [0, *(c * LANES for c in CUTS), width]
    return [(a, b - a) for a, b in zip(ends, ends[1:])]


def relation_copies(rel_hbm, rel_ref, sem):
    return [
        pltpu.make_async_copy(rel_hbm.at[:, pl.ds(a, n)], rel_ref.at[:, pl.ds(a, n)], sem.at[p])
        for p, (a, n) in enumerate(pieces_of(rel_hbm.shape[1]))
    ]


def relation_tile(rel_ref, ids, copies):
    total = None
    for p, (a, n) in enumerate(pieces_of(rel_ref.shape[1])):
        if copies is not None:
            copies[p].wait()
        term = dot(rel_ref[:, a : a + n], one_hot(ids, a, n))
        total = term if total is None else total + term
    return total


def relation_kernel(bucket, ids_ref, rel_hbm, out_ref, rel_ref, sem):
    copies = relation_copies(rel_hbm, rel_ref, sem)
    for copy in copies:
        copy.start()
    for t in range(ids_ref.shape[1] // TILE):
        cols = pl.ds(t * TILE, TILE)
        out_ref[:, cols] = relation_tile(rel_ref, ids_ref[bucket : bucket + 1, cols], None if t else copies).astype(BF)


def edge_tile(h, r, low, tails):
    half = h.shape[0] // 2
    h_re, h_im, r_re, r_im = h[:half], h[half:], r[:half], r[half:]
    q = jnp.concatenate([h_re * r_re - h_im * r_im, h_re * r_im + h_im * r_re], axis=0).astype(BF)
    t = jnp.tanh(0.5 * dot(low, q, ((0,), (0,))))
    at = lax.broadcasted_iota(jnp.int32, t.shape, 0) == tails
    k = 0.5 / low.shape[1]
    slopes = jnp.where(at, t * (k + 0.5) + (k - 0.5), t * k + k).astype(BF)
    g = dot(low, slopes)
    g_re, g_im = g[:half], g[half:]
    edge = jnp.concatenate([g_re * r_re + g_im * r_im, g_im * r_re - g_re * r_im], axis=0).astype(BF)
    return q, slopes, edge


def scatter(part_ref, edge_ref, hot_ref):
    width = part_ref.shape[2]
    for first in range(0, hot_ref.shape[0], SPAN):
        part = dot(edge_ref[...], hot_ref[first : first + SPAN, :], ((1,), (1,))).astype(BF)
        for n in range(SPAN // width):
            part_ref[first // width + n] = part[:, n * width : (n + 1) * width]


def stepped(table, state, grad):
    state_new = state + jnp.sum(grad * grad, axis=0, keepdims=True) * (1.0 / grad.shape[0])
    return table - (learning * lax.rsqrt(state_new)) * grad, state_new


def first_kernel(
    head_hbm, tail_hbm, rel_hbm, rows_hbm, tails_hbm, ids_hbm, state_ref, part_ref, tail_out, state_out, low_out,
    head_ref, tail_ref, rel_ref, rows_ref, tails_ref, ids_ref, hot_ref, low_ref, h_ref, edge_ref, q_ref, sl_ref, sem, rel_sem,
):
    pairs = [(ids_hbm, ids_ref), (rows_hbm, rows_ref), (head_hbm, head_ref), (tails_hbm, tails_ref), (tail_hbm, tail_ref)]
    copies = [pltpu.make_async_copy(a, b, sem.at[i]) for i, (a, b) in enumerate(pairs)]
    rel_copies = relation_copies(rel_hbm, rel_ref, rel_sem)
    for copy in copies[:1] + rel_copies + copies[1:]:
        copy.start()
    copies[0].wait()
    r = relation_tile(rel_ref, ids_ref[0:1, :], rel_copies)
    for copy in copies[1:]:
        copy.wait()
    hot_ref[...] = one_hot(rows_ref[0:1, :], 0, head_ref.shape[1])
    h = dot(head_ref[...].astype(BF), hot_ref[...])
    low_ref[...] = tail_ref[...].astype(BF)
    q_ref[...], sl_ref[...], edge_ref[...] = edge_tile(h, r, low_ref[...], tails_ref[0:1, :])
    tail, state_out[...] = stepped(tail_ref[...], state_ref[...], dot(q_ref[...], sl_ref[...], ((1,), (1,))))
    tail_ref[...] = tail
    low_ref[...] = tail.astype(BF)
    outs = [
        pltpu.make_async_copy(low_ref, low_out, sem.at[0]),
        pltpu.make_async_copy(tail_ref, tail_out, sem.at[1]),
    ]
    for copy in outs:
        copy.start()
    scatter(part_ref, edge_ref, hot_ref)
    for copy in outs:
        copy.wait()


def sum_kernel(got_ref, out_ref):
    total = got_ref[0].astype(F32)
    for n in range(1, got_ref.shape[0]):
        total = total + got_ref[n].astype(F32)
    total = total.astype(BF)
    for n in range(out_ref.shape[0]):
        out_ref[n] = total


def second_kernel(
    head_ref, state_ref, sums_ref, low_ref, rel_ref, rows_ref, tails_ref, part_ref, grad_out,
    head_low, hot_ref, edge_ref, q_ref, sl_ref,
):
    groups, _, width = sums_ref.shape
    for n in range(groups):
        cols = pl.ds(n * width, width)
        head_low[:, cols] = stepped(head_ref[:, cols], state_ref[:, cols], sums_ref[n].astype(F32))[0].astype(BF)
    hot_ref[...] = one_hot(rows_ref[1:2, :], 0, head_ref.shape[1])
    for t in range(rows_ref.shape[1] // TILE):
        cols = pl.ds(t * TILE, TILE)
        h = dot(head_low[...], hot_ref[:, cols])
        q_ref[:, cols], sl_ref[:, cols], edge_ref[:, cols] = edge_tile(
            h, rel_ref[:, cols].astype(F32), low_ref[...], tails_ref[1:2, cols]
        )
    scatter(part_ref, edge_ref, hot_ref)
    grad_out[...] = dot(q_ref[...], sl_ref[...], ((1,), (1,))).astype(BF)


def tail_end_kernel(tail_ref, state_ref, grad_ref, tail_out, state_out):
    tail_out[...], state_out[...] = stepped(tail_ref[...], state_ref[...], grad_ref[...].astype(F32))


def head_kernel(head_ref, state_ref, sums_ref, head_out, state_out):
    groups, _, width = sums_ref.shape
    for n in range(groups):
        cols = pl.ds(n * width, width)
        head_out[:, cols], state_out[:, cols] = stepped(
            head_ref[:, cols], state_ref[:, cols], sums_ref[n].astype(F32)
        )


def passed_along(value, axis, steps):
    count = lax.axis_size(axis)
    return lax.ppermute(value, axis, [(source, (source + steps) % count) for source in range(count)])


def spread(got, *before):
    same = call(sum_kernel, [(got.shape, BF)], [VMEM], (), 24, 0, 2 << 20)(got)[0]
    same, *before = lax.optimization_barrier((same, *before))
    return lax.all_to_all(same, "narrow", 0, 0, tiled=True), *before


def local(head_table, head_state, tail_table, tail_state, relations, head_rows, tail_rows, relation_ids):
    head, tail, rel = head_table.T, tail_table.T, relations.T
    h_state, t_state = head_state[None], tail_state[None]
    depth, hrows = head.shape
    types = rel.shape[1]
    trows = tail.shape[1]
    edges = head_rows.shape[1]
    groups = lax.axis_size("narrow")
    width = hrows // groups
    part_out = ((groups, depth, width), BF)
    edge_flops = 2 * depth * edges * (3 * trows + 2 * hrows)
    rel_flops = 2 * depth * types * edges
    ints = pltpu.VMEM(head_rows.shape, jnp.int32)
    hot = pltpu.VMEM((hrows, edges), BF)
    edge = pltpu.VMEM((depth, edges), BF)
    slope = pltpu.VMEM((trows, edges), BF)
    rel_scratch = pltpu.VMEM(rel.shape, BF)
    rel_sem = pltpu.SemaphoreType.DMA((PIECES,))

    part, tail, t_state, low = call(
        first_kernel, [part_out, (tail.shape, F32), ((1, trows), F32), (tail.shape, BF)], [ANY] * 6 + [VMEM],
        [
            pltpu.VMEM(head.shape, F32), pltpu.VMEM(tail.shape, F32), rel_scratch, ints, ints, ints,
            hot, pltpu.VMEM(tail.shape, BF), pltpu.VMEM((depth, edges), F32), edge, edge, slope,
            pltpu.SemaphoreType.DMA((5,)), rel_sem,
        ],
        60, edge_flops + rel_flops, 12 << 20, [VMEM, ANY, VMEM, ANY],
    )(head, tail, rel, head_rows, tail_rows, relation_ids, t_state)
    got = lax.all_to_all(part, "narrow", 0, 0, tiled=True)
    rel_1 = call(
        functools.partial(relation_kernel, 1), [((depth, edges), BF)], [VMEM, ANY], [rel_scratch, rel_sem],
        60, rel_flops, 2 * depth * types,
    )(relation_ids, rel)[0]
    moved = passed_along(low, "wide", 1)
    sums, moved, rel_1, tail, t_state = spread(got, moved, rel_1, tail, t_state)
    part, grad = call(
        second_kernel, [part_out, (tail.shape, BF)], [VMEM] * 7,
        [pltpu.VMEM(head.shape, BF), hot, edge, edge, slope],
        24, edge_flops, 9 << 20,
    )(head, h_state, sums, moved, rel_1, head_rows, tail_rows)
    got = lax.all_to_all(part, "narrow", 0, 0, tiled=True)
    grad = passed_along(grad, "wide", -1)
    head_step = call(
        head_kernel, [(head.shape, F32), ((1, hrows), F32)], [VMEM] * 3, (), 24, 0, 4 << 20
    )
    head, h_state = head_step(head, h_state, sums)
    tail, t_state = call(
        tail_end_kernel, [(tail.shape, F32), ((1, trows), F32)], [VMEM] * 3, (), 24, 0, 2 << 20
    )(tail, t_state, grad)
    sums, tail, t_state, head, h_state = spread(got, tail, t_state, head, h_state)
    head, h_state = head_step(head, h_state, sums)
    return head.T, h_state[0], tail.T, t_state[0]


def solution(mesh):
    return jax.shard_map(
        local,
        mesh=mesh,
        in_specs=(
            P("wide", None),
            P("wide"),
            P(("wide", "narrow"), None),
            P(("wide", "narrow")),
            P(),
            P(None, ("wide", "narrow")),
            P(None, ("wide", "narrow")),
            P(None, ("wide", "narrow")),
        ),
        out_specs=(P("wide", None), P("wide"), P(("wide", "narrow"), None), P(("wide", "narrow"))),
        check_vma=False,
    )
```
